256 devices in a mesh: chan: 64 (over y, z, x_lo), win: 4 (over x_hi, core).
Axes of the slice: x: 4 (x_hi: 2, x_lo: 2; x = x_hi * 2 + x_lo), y: 4, z: 8, core: 2. Of those that a mesh axis runs over, the one named last changes fastest.
Arguments:
- source_spectra: bfloat16 [64, 256, 8, 2048], P('chan', None, 'win'), may hold values from -6 to 6
- receiver_spectra: bfloat16 [512, 8, 2048], P('chan', 'win'), may hold values from -6 to 6
- block_order: int32 [2], replicated, may hold values from 0 to 63
- source_mask: int32 [64, 256], P('chan'), may hold values 0 or 1
- receiver_mask: int32 [512], P('chan'), may hold values 0 or 1
Outputs:
- correlations: bfloat16 [2, 256, 512, 2048], P(None, 'win', 'chan')
The draws below stay inside these ranges and needn't reach their ends.
All inputs are finite; a program needn't handle non-finite values. No bound on the sum of `source_mask` or of `receiver_mask` on one device may be relied on, other than what follows from the above.
Results may differ from the reference program's by a relative error of at most 0.0058.
Values may be sent and summed in bfloat16 or wider, within the bound.
No kernel may reach another device: no remote copies, remote signals or barrier semaphores. Data moves between devices by JAX's collectives and lax.ppermute only.
A program may use at most 192 MiB of HBM per device.

```python
import math
import jax
import jax.numpy as jnp
from jax import lax

F = 1024
S = 256
RECV_DEV = 8
STEPS = 2
NLAG = 2048
WINDOWS = 8
RECV = 512
BLOCKS = 64


def set_ends(result, rng, least, largest):
    index_at = [jax.random.randint(jax.random.fold_in(rng, axis), (), 0, length) for axis, length in enumerate(result.shape)]
    main_axis = result.shape.index(max(result.shape))
    beside = index_at[:main_axis] + [(index_at[main_axis] + 1) % result.shape[main_axis]] + index_at[main_axis + 1:]
    return result.at[tuple(index_at)].set(least).at[tuple(beside)].set(largest)


def shard_levels(own_key, shape, split, low, high):
    gain, own = 1.0, jax.random.fold_in(own_key, 6)
    for position, parts in split:
        draws = jnp.exp(jax.random.uniform(jax.random.fold_in(own, position), (parts,), jnp.float32, low / len(split), high / len(split)))
        gain = gain * jnp.repeat(draws, shape[position] // parts).reshape([-1 if axis == position else 1 for axis in range(len(shape))])
    return gain


def gaussian(rng, extent, scale, most, shards=(), held_as=jnp.bfloat16):
    result = jax.random.normal(rng, extent, jnp.float32) * scale
    if len(shards) > 0:
        result = shard_levels(rng, extent, shards, -0.22, 0.18) * result
    return jnp.clip(result, min=-most, max=most).astype(held_as)


def setup_inputs(seed: int = 0) -> dict:
    splits = jax.random.split(jax.random.key(seed), 6)
    source_spectra = gaussian(splits[0], (BLOCKS, S, WINDOWS, 2 * F), 1.0, 6.0, ((0, 64), (2, 4)))
    receiver_spectra = gaussian(splits[1], (RECV, WINDOWS, 2 * F), 1.0, 6.0, ((0, 64), (1, 4)))
    block_order = jax.random.randint(splits[2], (STEPS,), 0, BLOCKS).astype(jnp.int32)
    source_mask = set_ends((jax.random.randint(splits[3], (BLOCKS, S), 0, 8) < 7).astype(jnp.int32), jax.random.fold_in(splits[3], 1), 0, 1)
    receiver_mask = set_ends((jax.random.randint(splits[4], (RECV,), 0, 8) < 7).astype(jnp.int32), jax.random.fold_in(splits[4], 1), 0, 1)
    return {"source_spectra": source_spectra, "receiver_spectra": receiver_spectra, "block_order": block_order, "source_mask": source_mask, "receiver_mask": receiver_mask}


def lag_table(freqs):
    nfft = 2 * freqs
    bins = jnp.arange(freqs, dtype=jnp.int32)[:, None]
    lags = jnp.arange(nfft, dtype=jnp.int32)[None, :] - freqs
    phase = jnp.mod(bins * lags, nfft).astype(jnp.float32) * (2.0 * math.pi / nfft)
    weight = jnp.where(bins == 0, 1.0, 2.0).astype(jnp.float32) / math.sqrt(nfft)
    table = jnp.concatenate([weight * jnp.cos(phase), -weight * jnp.sin(phase)], axis=0)
    return table.astype(jnp.bfloat16)

def cross_sum(sources, receivers):
    half = sources.shape[2] // 2
    s_re = sources[..., :half].astype(jnp.float32)
    s_im = sources[..., half:].astype(jnp.float32)
    r_re = receivers[..., :half].astype(jnp.float32)
    r_im = receivers[..., half:].astype(jnp.float32)
    real = jnp.einsum('swk,rwk->srk', s_re, r_re) + jnp.einsum('swk,rwk->srk', s_im, r_im)
    imag = jnp.einsum('swk,rwk->srk', s_re, r_im) - jnp.einsum('swk,rwk->srk', s_im, r_re)
    return jnp.concatenate([real, imag], axis=-1)

def reference(source_spectra, receiver_spectra, block_order, source_mask, receiver_mask):
    table = lag_table(F)
    table_wide = table.astype(jnp.float32)
    receivers = receiver_spectra * receiver_mask[:, None, None].astype(jnp.bfloat16)
    groups = receivers.reshape(RECV // RECV_DEV, RECV_DEV, WINDOWS, 2 * F)
    results = []
    for step in range(STEPS):
        chosen = block_order[step]
        block = lax.dynamic_index_in_dim(source_spectra, chosen, 0, keepdims=False)
        keep = lax.dynamic_index_in_dim(source_mask, chosen, 0, keepdims=False)
        block = block * keep[:, None, None].astype(jnp.bfloat16)

        def one_group(group):
            stack = (cross_sum(block, group) / WINDOWS).astype(jnp.bfloat16)
            rows = stack.reshape(S * RECV_DEV, 2 * F).astype(jnp.float32)
            corr = jnp.dot(rows, table_wide, preferred_element_type=jnp.float32)
            return corr.astype(jnp.bfloat16).reshape(S, RECV_DEV, NLAG)
        mapped = lax.map(one_group, groups)
        results.append(jnp.transpose(mapped, (1, 0, 2, 3)).reshape(S, RECV, NLAG))
    return jnp.stack(results)
```

```python
import functools
import math

import jax
import jax.numpy as jnp
from jax import lax
from jax.experimental import pallas as pl
from jax.experimental.pallas import tpu as pltpu
from jax.sharding import PartitionSpec as P

NY, NZ, NX = 4, 8, 2


def chan_pairs(dy, dz, dx):
    pairs = []
    for y in range(NY):
        for z in range(NZ):
            for x in range(NX):
                target = (((y + dy) % NY) * NZ + (z + dz) % NZ) * NX + (x + dx) % NX
                pairs.append(((y * NZ + z) * NX + x, target))
    return pairs


def shift(value, dy=0, dz=0, dx=0):
    return lax.ppermute(value, "chan", chan_pairs(dy, dz, dx))


def half_table(freqs, parity):
    nfft = 2 * freqs
    bins = 2 * jnp.arange(freqs // 2, dtype=jnp.int32)[:, None] + parity
    lags = jnp.arange(freqs, dtype=jnp.int32)[None, :] - freqs
    phase = jnp.mod(bins * lags, nfft).astype(jnp.float32) * (2.0 * math.pi / nfft)
    weight = jnp.where(bins == 0, 1.0, 2.0).astype(jnp.float32) / math.sqrt(nfft)
    table = jnp.concatenate([weight * jnp.cos(phase), -weight * jnp.sin(phase)], axis=0)
    return table.astype(jnp.bfloat16)


def split_matrix(width):
    row = jnp.arange(width, dtype=jnp.int32)[:, None]
    column = jnp.arange(width, dtype=jnp.int32)[None, :]
    half = width // 2
    source = jnp.where(column < half, 2 * column, 2 * (column - half) + 1)
    return (row == source).astype(jnp.bfloat16)


def corr_kernel(n_pieces, windows, place, *refs):
    pieces = refs[:n_pieces]
    receivers, split, even, odd = refs[n_pieces : n_pieces + 4]
    out, wide, cross = refs[-3:]
    freqs = even.shape[1]
    lane = 128
    scale = 1.0 / windows
    x = place[place.shape[0] - 1]
    wide[...] = receivers[...].astype(jnp.float32)
    at = 0
    for piece in pieces:
        pairs = piece.shape[0] // 2

        def one_pair(i, _, piece=piece, at=at):
            row = pl.multiple_of(place[at + i] * 16, 16)
            for tile in range(freqs // lane):
                re = pl.ds(tile * lane, lane)
                im = pl.ds(freqs + tile * lane, lane)
                halves_re, halves_im = [], []
                for parity in range(2):
                    spectrum = piece.at[2 * i + (x + parity) % 2]
                    s_re = spectrum[:, re].astype(jnp.float32)
                    s_im = spectrum[:, im].astype(jnp.float32)
                    real = imag = None
                    for w in range(windows):
                        a = jnp.broadcast_to(s_re[w : w + 1], (8, lane))
                        b = jnp.broadcast_to(s_im[w : w + 1], (8, lane))
                        c = wide[w, :, re]
                        d = wide[w, :, im]
                        p = a * c + b * d
                        q = a * d - b * c
                        real = p if real is None else real + p
                        imag = q if imag is None else imag + q
                    halves_re.append(real)
                    halves_im.append(imag)
                cross[pl.ds(row, 16), re] = (jnp.concatenate(halves_re) * scale).astype(jnp.bfloat16)
                cross[pl.ds(row, 16), im] = (jnp.concatenate(halves_im) * scale).astype(jnp.bfloat16)
            return 0

        lax.fori_loop(0, pairs, one_pair, 0)
        at += pairs
    rows = cross.shape[0]
    block = split.shape[0]
    part = 256

    def some_rows(i, _):
        at_rows = pl.ds(pl.multiple_of(i * part, part), part)
        evens, odds = [], []
        for k in range(cross.shape[1] // block):
            both = jnp.dot(cross[at_rows, pl.ds(k * block, block)], split[...], preferred_element_type=jnp.float32).astype(jnp.bfloat16)
            evens.append(both[:, : block // 2])
            odds.append(both[:, block // 2 :])
        lhs_even = jnp.concatenate(evens, axis=1)
        lhs_odd = jnp.concatenate(odds, axis=1)
        for n in range(freqs // 256):
            columns = pl.ds(n * 256, 256)
            e = jnp.dot(lhs_even, even[:, columns], preferred_element_type=jnp.float32)
            o = jnp.dot(lhs_odd, odd[:, columns], preferred_element_type=jnp.float32)
            out[at_rows, columns] = (e + o).astype(jnp.bfloat16)
            out[at_rows, pl.ds(freqs + n * 256, 256)] = (e - o).astype(jnp.bfloat16)
        return 0

    lax.fori_loop(0, rows // part, some_rows, 0)


def correlate(step, steps, place, pieces, receivers, split, even, odd, *result):
    windows, r, width = receivers.shape
    rows = sum(piece.shape[0] for piece in pieces) * r
    whole = pl.BlockSpec(memory_space=pltpu.VMEM)
    return pl.pallas_call(
        functools.partial(corr_kernel, len(pieces), windows),
        grid=(1,),
        out_shape=jax.ShapeDtypeStruct((steps * rows, width), jnp.bfloat16),
        in_specs=[pl.BlockSpec(memory_space=pltpu.SMEM)] + [whole] * (len(pieces) + 4) + [pl.BlockSpec(memory_space=pl.ANY)] * len(result),
        out_specs=pl.BlockSpec((rows, width), lambda i: (step, 0)),
        scratch_shapes=[
            pltpu.VMEM((windows, r, width), jnp.float32),
            pltpu.VMEM((rows, width), jnp.bfloat16),
        ],
        input_output_aliases={len(pieces) + 5: 0} if result else {},
        compiler_params=pltpu.CompilerParams(vmem_limit_bytes=40 * 1024 * 1024),
        cost_estimate=pl.CostEstimate(flops=6 * 10**9, bytes_accessed=10 * 2**20, transcendentals=0),
        name=f"correlate_{step}",
    )(place, *pieces, receivers, split, even, odd, *result)


def on_device(source_spectra, receiver_spectra, block_order, source_mask, receiver_mask):
    width = receiver_spectra.shape[2]
    freqs = width // 2
    own_windows = receiver_spectra.shape[1]
    r = receiver_spectra.shape[0]
    wins = lax.axis_size("win")
    chans = lax.axis_size("chan")
    windows = own_windows * wins
    steps = block_order.shape[0]
    me = lax.axis_index("chan")
    win = lax.axis_index("win")
    y, z, x = me // (NZ * NX), (me // NX) % NZ, me % NX

    owned = source_spectra[0] * source_mask[0][:, None, None].astype(jnp.bfloat16)
    rows = owned.reshape(wins, chans, own_windows, width).transpose(1, 0, 2, 3)
    spread = lax.all_to_all(rows.reshape(chans, wins * own_windows, width), "chan", 0, 0, tiled=True)

    def over_win(give):
        kept = [give(win)]
        for j in range(1, wins):
            kept.append(lax.ppermute(give(win ^ j), "win", [(w, w ^ j) for w in range(wins)]))
        return kept

    receivers = receiver_spectra * receiver_mask[:, None, None].astype(jnp.bfloat16)
    receivers = receivers.transpose(1, 0, 2)
    receivers = jnp.concatenate(over_win(lambda to: receivers), axis=0)

    chosen = jnp.stack([lax.dynamic_index_in_dim(spread, block_order[t], 0, keepdims=False) for t in range(steps)])
    chosen = chosen.reshape(steps, wins, own_windows, width)
    mine = jnp.concatenate(over_win(lambda to: lax.dynamic_index_in_dim(chosen, to, 1, keepdims=False)), axis=1)

    other = shift(mine, dx=1)
    pair = jnp.stack([mine, other], axis=1)
    first, second = pair[0], pair[1]
    y_off = (0, 1, 3, 2)
    z_off = (0, 1, 7, 2, 6, 3, 5, 4)
    first = jnp.concatenate([first] + [shift(first, dy=k) for k in y_off[1:]])
    second = jnp.concatenate([second] + [shift(second, dz=k) for k in z_off[1:]])
    second_pieces = [second] + [shift(second, dy=k) for k in y_off[1:]]
    first_pieces = [first]
    up = down = first
    for k in range(1, 5):
        up = shift(up, dz=1)
        first_pieces.append(up)
        if k < 4:
            down = shift(down, dz=-1)
            first_pieces.append(down)

    ys = jnp.mod(y - jnp.array(y_off, jnp.int32), NY)
    zs = jnp.mod(z - jnp.array(z_off, jnp.int32), NZ)
    place_first = jnp.append((ys[None, :] * NZ + zs[:, None]).reshape(-1), x)
    place_second = jnp.append((ys[:, None] * NZ + zs[None, :]).reshape(-1), x)

    split = split_matrix(256)
    even = half_table(freqs, 0)
    odd = half_table(freqs, 1)
    result = correlate(0, steps, place_first, first_pieces, receivers, split, even, odd)
    result = correlate(1, steps, place_second, second_pieces, receivers, split, even, odd, result)
    return result.reshape(steps, chans, r, width)


def solution(mesh):
    return jax.shard_map(
        on_device,
        mesh=mesh,
        in_specs=(
            P("chan", None, "win", None),
            P("chan", "win", None),
            P(),
            P("chan", None),
            P("chan"),
        ),
        out_specs=P(None, "win", "chan", None),
        check_vma=False,
    )
```

```python
import functools
import math

import jax
import jax.numpy as jnp
from jax import lax
from jax.experimental import pallas as pl
from jax.experimental.pallas import tpu as pltpu
from jax.sharding import PartitionSpec as P

NY, NZ, NX = 4, 8, 2
BF16 = jnp.bfloat16
F32 = jnp.float32


def chan_index(y, z, x):
    return ((y % NY) * NZ + z % NZ) * NX + x % NX


def shift(value, dy=0, dz=0, dx=0):
    pairs = []
    for y in range(NY):
        for z in range(NZ):
            for x in range(NX):
                pairs.append((chan_index(y, z, x), chan_index(y + dy, z + dz, x + dx)))
    return lax.ppermute(value, "chan", pairs)


def yx_groups():
    return [[chan_index(y, z, x) for y in range(NY) for x in range(NX)] for z in range(NZ)]


def z_groups():
    return [[chan_index(y, z, x) for z in range(NZ)] for y in range(NY) for x in range(NX)]


def yx_win_groups(wins):
    return [[chan * wins + w for chan in group for w in range(wins)] for group in yx_groups()]


def half_table(freqs, parity):
    nfft = 2 * freqs
    bins = 2 * jnp.arange(freqs // 2, dtype=jnp.int32)[:, None] + parity
    lags = jnp.arange(freqs, dtype=jnp.int32)[None, :] - freqs
    phase = jnp.mod(bins * lags, nfft).astype(F32) * (2.0 * math.pi / nfft)
    weight = jnp.where(bins == 0, 1.0, 2.0).astype(F32) / math.sqrt(nfft)
    table = jnp.concatenate([weight * jnp.cos(phase), -weight * jnp.sin(phase)], axis=0)
    return table.astype(BF16)


def split_matrix(width):
    row = jnp.arange(width, dtype=jnp.int32)[:, None]
    column = jnp.arange(width, dtype=jnp.int32)[None, :]
    half = width // 2
    source = jnp.where(column < half, 2 * column, 2 * (column - half) + 1)
    return (row == source).astype(BF16)


def add_cross(piece, receivers, wide, cross, first_pair):
    windows, r, width = receivers.shape
    freqs = width // 2
    lane = 128
    scale = 1.0 / windows

    def one_pair(i, _, step):
        row = pl.multiple_of((first_pair + step * (piece.shape[0] // 2) + i) * 2 * r, 2 * r)
        wide[...] = piece[pl.ds(2 * i, 2), step * windows : (step + 1) * windows].astype(F32)
        for tile in range(freqs // lane):
            re = pl.ds(tile * lane, lane)
            im = pl.ds(freqs + tile * lane, lane)
            real, imag = [None, None], [None, None]
            for w in range(windows):
                c, d = receivers[w, :, re], receivers[w, :, im]
                for member in range(2):
                    a = jnp.broadcast_to(wide[member, w : w + 1, re], c.shape)
                    b = jnp.broadcast_to(wide[member, w : w + 1, im], c.shape)
                    p, q = a * c + b * d, a * d - b * c
                    real[member] = p if w == 0 else real[member] + p
                    imag[member] = q if w == 0 else imag[member] + q
            cross[pl.ds(row, 2 * r), re] = (jnp.concatenate(real) * scale).astype(BF16)
            cross[pl.ds(row, 2 * r), im] = (jnp.concatenate(imag) * scale).astype(BF16)
        return 0

    for step in range(piece.shape[1] // windows):
        lax.fori_loop(0, piece.shape[0] // 2, functools.partial(one_pair, step=step), 0)


def lag_kernel(n_pieces, first_place, place, *refs):
    pieces = refs[:n_pieces]
    receivers, split, even_in, odd_in = refs[n_pieces : n_pieces + 4]
    out, wide, cross, result, even, odd, table_sem, sem = refs[-8:]
    tables = [
        pltpu.make_async_copy(even_in, even, table_sem.at[0]),
        pltpu.make_async_copy(odd_in, odd, table_sem.at[1]),
    ]
    for copy in tables:
        copy.start()
    freqs = even.shape[1]
    pair = 2 * receivers.shape[1]
    at = 0
    for piece in pieces:
        add_cross(piece, receivers, wide, cross, at)
        at += piece.shape[0] * piece.shape[1] // (2 * receivers.shape[0])
    for copy in tables:
        copy.wait()
    block = split.shape[0]
    total = at * pair
    chunk = 256 if total % 256 == 0 else 192 if total % 192 == 0 else total
    copies = []
    for first in range(0, total, chunk):
        rows = pl.ds(first, chunk)
        evens, odds = [], []
        for k in range(cross.shape[1] // block):
            both = jnp.dot(cross[rows, pl.ds(k * block, block)], split[...], preferred_element_type=F32).astype(BF16)
            evens.append(both[:, : block // 2])
            odds.append(both[:, block // 2 :])
        lhs_even = jnp.concatenate(evens, axis=1)
        lhs_odd = jnp.concatenate(odds, axis=1)
        for n in range(freqs // 256):
            columns = pl.ds(n * 256, 256)
            e = jnp.dot(lhs_even, even[:, columns], preferred_element_type=F32)
            o = jnp.dot(lhs_odd, odd[:, columns], preferred_element_type=F32)
            result[rows, columns] = (e + o).astype(BF16)
            result[rows, pl.ds(freqs + n * 256, 256)] = (e - o).astype(BF16)
        for i in range(first // pair, (first + chunk) // pair):
            row = pl.multiple_of(place[first_place + i] * pair, pair)
            copy = pltpu.make_async_copy(result.at[pl.ds(i * pair, pair)], out.at[pl.ds(row, pair)], sem.at[i])
            copy.start()
            copies.append(copy)
    for copy in copies:
        copy.wait()


def lags_of(name, place, first_place, pieces, receivers, split, even, odd, out_rows, *result):
    windows, r, width = receivers.shape
    rows = sum(piece.shape[0] * piece.shape[1] for piece in pieces) * r // windows
    whole = pl.BlockSpec(memory_space=pltpu.VMEM)
    anywhere = pl.BlockSpec(memory_space=pl.ANY)
    in_hbm = pl.BlockSpec(memory_space=pltpu.HBM)
    held = len(pieces)
    return pl.pallas_call(
        functools.partial(lag_kernel, len(pieces), first_place),
        out_shape=jax.ShapeDtypeStruct((out_rows, width), BF16),
        in_specs=[pl.BlockSpec(memory_space=pltpu.SMEM)] + [whole] * (held + 2) + [in_hbm] * 2 + [anywhere] * len(result),
        out_specs=anywhere,
        scratch_shapes=[
            pltpu.VMEM((2, windows, width), F32),
            pltpu.VMEM((rows, width), BF16),
            pltpu.VMEM((rows, width), BF16),
            pltpu.VMEM(even.shape, BF16),
            pltpu.VMEM(odd.shape, BF16),
            pltpu.SemaphoreType.DMA((2,)),
            pltpu.SemaphoreType.DMA((rows // (2 * r),)),
        ],
        input_output_aliases={held + 5: 0} if result else {},
        compiler_params=pltpu.CompilerParams(vmem_limit_bytes=16 * 1024 * 1024),
        cost_estimate=pl.CostEstimate(flops=rows * 12 * 10**6, bytes_accessed=rows * 2**14, transcendentals=0),
        name=name,
    )(place, *pieces, receivers, split, even, odd, *result)


def on_device(source_spectra, receiver_spectra, block_order, source_mask, receiver_mask):
    width = receiver_spectra.shape[2]
    freqs = width // 2
    r, own_windows = receiver_spectra.shape[:2]
    wins = lax.axis_size("win")
    chans = lax.axis_size("chan")
    windows = own_windows * wins
    steps = block_order.shape[0]
    me = lax.axis_index("chan")
    win = lax.axis_index("win")
    z = (me // NX) % NZ

    owned = source_spectra[0] * source_mask[0][:, None, None].astype(BF16)
    rows = owned.reshape(wins, NY, NZ, NX, own_windows, width).transpose(1, 3, 0, 2, 4, 5)
    rows = rows.reshape(NY * NX * wins, NZ * own_windows, width)
    rows, receiver_spectra = lax.optimization_barrier((rows, receiver_spectra))
    spread = lax.all_to_all(rows, ("chan", "win"), 0, 0, tiled=True, axis_index_groups=yx_win_groups(wins))

    def all_windows(give):
        kept = [give(win)]
        for j in range(1, wins):
            kept.append(lax.ppermute(give(jnp.mod(win + j, wins)), "win", [(w, (w + j) % wins) for w in range(wins)]))
        return jnp.concatenate([lax.select_n(jnp.mod(win - w, wins), *kept) for w in range(wins)], axis=0)

    split = split_matrix(256)
    even = half_table(freqs, 0)
    odd = half_table(freqs, 1)
    receivers = receiver_spectra * receiver_mask[:, None, None].astype(BF16)
    receivers = all_windows(lambda to: receivers.transpose(1, 0, 2)).astype(F32)

    ys = jnp.arange(NY, dtype=jnp.int32)
    zs = jnp.mod(z - jnp.array((0, 1, -1, 2, -2, 3, -3), jnp.int32), NZ)
    bases = (jnp.arange(steps, dtype=jnp.int32)[:, None] * (NY * NZ) + (ys * NZ)[None, :]).reshape(1, -1)
    last = (bases + jnp.mod(z + NZ // 2, NZ)).reshape(steps, 2, NY // 2).transpose(1, 0, 2)
    place = jnp.concatenate([(bases + zs[:, None]).reshape(-1), last.reshape(-1)])
    owner_y, owner_z, owner_x = block_order // (NZ * NX), (block_order // NX) % NZ, block_order % NX
    first_from = [(owner_y[t] * NX + owner_x[t]) * wins for t in range(steps)]
    owner_z = [owner_z[t] for t in range(steps)]
    shadow = (receivers, split, even, odd, place, first_from, owner_z)
    spread, shadow = lax.optimization_barrier((spread, shadow))
    receivers, split, even, odd, place, first_from, owner_z = shadow

    chosen = [lax.dynamic_slice_in_dim(spread, first_from[t], wins, 0) for t in range(steps)]
    chosen = jnp.stack([part.reshape(wins, NZ, own_windows, width) for part in chosen])
    chosen = chosen.transpose(2, 0, 1, 3, 4).reshape(NZ, steps * windows, width)
    chosen = lax.all_to_all(chosen, "chan", 0, 0, tiled=True, axis_index_groups=z_groups())
    chosen = [lax.dynamic_index_in_dim(chosen, owner_z[t], 0, keepdims=False) for t in range(steps)]
    chosen = jnp.concatenate([part[t * windows : (t + 1) * windows] for t, part in enumerate(chosen)])

    def gather_yx(value):
        copies = jnp.broadcast_to(value[None], (NY * NX,) + value.shape)
        return lax.all_to_all(copies, "chan", 0, 0, tiled=True, axis_index_groups=yx_groups())

    near = gather_yx(chosen)

    tables = (receivers, split, even, odd, steps * chans * r)
    up, down = shift(near, dz=1), shift(near, dz=-1)
    up2, down2 = shift(up, dz=1), shift(down, dz=-1)
    pairs = steps * NY
    half = near.shape[0] // 2
    out = lags_of("lags_a", place, 0, (near, up, down), *tables)
    up2, down2, out = lax.optimization_barrier((up2, down2, out))
    up3, down3 = shift(up2, dz=1), shift(down2, dz=-1)
    out = lags_of("lags_b", place, 3 * pairs, (up2, down2), *tables, out)
    up3, down3, out = lax.optimization_barrier((up3, down3, out))
    up4, down4 = shift(up3[:half], dz=1), shift(down3[half:], dz=-1)
    out = lags_of("lags_c", place, 5 * pairs, (up3, down3), *tables, out)
    up4, down4, out = lax.optimization_barrier((up4, down4, out))
    out = lags_of("lags_d", place, 7 * pairs, (up4, down4), *tables, out)
    return out.reshape(steps, chans, r, width)


def solution(mesh):
    return jax.shard_map(
        on_device,
        mesh=mesh,
        in_specs=(
            P("chan", None, "win", None),
            P("chan", "win", None),
            P(),
            P("chan", None),
            P("chan"),
        ),
        out_specs=P(None, "win", "chan", None),
        check_vma=False,
    )
```

```python
import functools
import math

import jax
import jax.numpy as jnp
from jax import lax
from jax.experimental import pallas as pl
from jax.experimental.pallas import tpu as pltpu
from jax.sharding import PartitionSpec as P

NY, NZ, NX = 4, 8, 2
BF16 = jnp.bfloat16
F32 = jnp.float32


def chan_index(y, z, x):
    return ((y % NY) * NZ + z % NZ) * NX + x % NX


def shift(value, dy=0, dz=0, dx=0):
    pairs = []
    for y in range(NY):
        for z in range(NZ):
            for x in range(NX):
                pairs.append((chan_index(y, z, x), chan_index(y + dy, z + dz, x + dx)))
    return lax.ppermute(value, "chan", pairs)


def yx_groups():
    return [[chan_index(y, z, x) for y in range(NY) for x in range(NX)] for z in range(NZ)]


def z_groups():
    return [[chan_index(y, z, x) for z in range(NZ)] for y in range(NY) for x in range(NX)]


def yx_win_groups(wins):
    return [[chan * wins + w for chan in group for w in range(wins)] for group in yx_groups()]


def half_table(freqs, parity):
    nfft = 2 * freqs
    bins = 2 * jnp.arange(freqs // 2, dtype=jnp.int32)[:, None] + parity
    lags = jnp.arange(freqs, dtype=jnp.int32)[None, :] - freqs
    phase = jnp.mod(bins * lags, nfft).astype(F32) * (2.0 * math.pi / nfft)
    weight = jnp.where(bins == 0, 1.0, 2.0).astype(F32) / math.sqrt(nfft)
    table = jnp.concatenate([weight * jnp.cos(phase), -weight * jnp.sin(phase)], axis=0)
    return table.astype(BF16)


def split_matrix(width):
    row = jnp.arange(width, dtype=jnp.int32)[:, None]
    column = jnp.arange(width, dtype=jnp.int32)[None, :]
    half = width // 2
    source = jnp.where(column < half, 2 * column, 2 * (column - half) + 1)
    return (row == source).astype(BF16)


def add_cross(piece, receivers, wide, cross, first_pair):
    windows, r, width = receivers.shape
    freqs = width // 2
    lane = 128
    scale = 1.0 / windows

    def one_pair(i, _, step):
        row = pl.multiple_of((first_pair + step * (piece.shape[0] // 2) + i) * 2 * r, 2 * r)
        wide[...] = piece[pl.ds(2 * i, 2), step * windows : (step + 1) * windows].astype(F32)
        for tile in range(freqs // lane):
            re = pl.ds(tile * lane, lane)
            im = pl.ds(freqs + tile * lane, lane)
            real, imag = [None, None], [None, None]
            for w in range(windows):
                c, d = receivers[w, :, re], receivers[w, :, im]
                for member in range(2):
                    a = jnp.broadcast_to(wide[member, w : w + 1, re], c.shape)
                    b = jnp.broadcast_to(wide[member, w : w + 1, im], c.shape)
                    p, q = a * c + b * d, a * d - b * c
                    real[member] = p if w == 0 else real[member] + p
                    imag[member] = q if w == 0 else imag[member] + q
            cross[pl.ds(row, 2 * r), re] = (jnp.concatenate(real) * scale).astype(BF16)
            cross[pl.ds(row, 2 * r), im] = (jnp.concatenate(imag) * scale).astype(BF16)
        return 0

    for step in range(piece.shape[1] // windows):
        lax.fori_loop(0, piece.shape[0] // 2, functools.partial(one_pair, step=step), 0)


def fetch(refs, buffers, sems):
    copies = [pltpu.make_async_copy(ref, buffer, sems.at[i]) for i, (ref, buffer) in enumerate(zip(refs, buffers))]
    for copy in copies:
        copy.start()
    return copies


def in_hbm(array):
    return pltpu.with_memory_space_constraint(array, pltpu.HBM)


def buffers_of(arrays):
    return [pltpu.VMEM(array.shape, array.dtype) for array in arrays] + [pltpu.SemaphoreType.DMA((len(arrays),))]


def cross_kernel(*refs):
    n = (len(refs) - 7) // 2
    sources, out = refs[: n + 1], refs[n + 1]
    buffers, (sems, cross, wide, sem) = refs[n + 2 : 2 * n + 3], refs[2 * n + 3 :]
    copies = fetch(sources, buffers, sems)
    copies[0].wait()
    receivers, pieces = buffers[0], buffers[1:]
    at = 0
    for piece, copy in zip(pieces, copies[1:]):
        copy.wait()
        add_cross(piece, receivers, wide, cross, at)
        at += piece.shape[0] * piece.shape[1] // (2 * receivers.shape[0])
    copy = pltpu.make_async_copy(cross, out, sem)
    copy.start()
    copy.wait()


def cross_rows(pieces, receivers):
    return sum(piece.shape[0] * piece.shape[1] for piece in pieces) * receivers.shape[1] // receivers.shape[0]


def cross_of(name, pieces, receivers):
    windows, r, width = receivers.shape
    rows = cross_rows(pieces, receivers)
    anywhere = pl.BlockSpec(memory_space=pl.ANY)
    inputs = (in_hbm(receivers), *pieces)
    return pl.pallas_call(
        cross_kernel,
        out_shape=pltpu.HBM((rows, width), BF16),
        in_specs=[anywhere] * len(inputs),
        out_specs=anywhere,
        scratch_shapes=buffers_of(inputs)
        + [pltpu.VMEM((rows, width), BF16), pltpu.VMEM((2, windows, width), F32), pltpu.SemaphoreType.DMA],
        compiler_params=pltpu.CompilerParams(vmem_limit_bytes=8 * 1024 * 1024),
        cost_estimate=pl.CostEstimate(flops=rows * 10**6, bytes_accessed=rows * 2**10, transcendentals=0),
        name=name,
    )(*inputs)


def lag_kernel(n_done, n_pieces, first_place, aliased, place, *refs):
    n = n_done + n_pieces + 4
    sources, refs = refs[:n], refs[n + aliased :]
    out, buffers, (sems, wide, cross, result, sem) = refs[0], refs[1 : n + 1], refs[n + 1 :]
    receivers, pieces, split = buffers[0], buffers[1 : 1 + n_pieces], buffers[1 + n_pieces + n_done]
    even, odd = buffers[-2:]
    spans = []
    at = 0
    pair = 2 * receivers.shape[1]
    for part in buffers[1 + n_pieces : 1 + n_pieces + n_done]:
        spans.append(cross.at[pl.ds(at * pair, part.shape[0])])
        at += part.shape[0] // pair
    targets = list(buffers)
    targets[1 + n_pieces : 1 + n_pieces + n_done] = spans
    copies = fetch(sources, targets, sems)
    copies[0].wait()
    for piece, copy in zip(pieces, copies[1:]):
        copy.wait()
        add_cross(piece, receivers, wide, cross, at)
        at += piece.shape[0] * piece.shape[1] // (2 * receivers.shape[0])
    for copy in copies[1 + n_pieces :]:
        copy.wait()
    freqs = even.shape[1]
    block = split.shape[0]
    total = at * pair
    chunk = 192 if total % 192 == 0 else 256
    copies = []
    for first in range(0, total, chunk):
        rows = pl.ds(first, chunk)
        evens, odds = [], []
        for k in range(cross.shape[1] // block):
            both = jnp.dot(cross[rows, pl.ds(k * block, block)], split[...], preferred_element_type=F32).astype(BF16)
            evens.append(both[:, : block // 2])
            odds.append(both[:, block // 2 :])
        lhs_even = jnp.concatenate(evens, axis=1)
        lhs_odd = jnp.concatenate(odds, axis=1)
        for n in range(freqs // 256):
            columns = pl.ds(n * 256, 256)
            e = jnp.dot(lhs_even, even[:, columns], preferred_element_type=F32)
            o = jnp.dot(lhs_odd, odd[:, columns], preferred_element_type=F32)
            result[rows, columns] = (e + o).astype(BF16)
            result[rows, pl.ds(freqs + n * 256, 256)] = (e - o).astype(BF16)
        for i in range(first // pair, (first + chunk) // pair):
            row = pl.multiple_of(place[first_place + i] * pair, pair)
            copy = pltpu.make_async_copy(result.at[pl.ds(i * pair, pair)], out.at[pl.ds(row, pair)], sem.at[i])
            copy.start()
            copies.append(copy)
    for copy in copies:
        copy.wait()


def lags_of(name, place, first_place, done, pieces, receivers, split, even, odd, out_rows, *result):
    windows, r, width = receivers.shape
    rows = cross_rows(pieces, receivers) + sum(part.shape[0] for part in done)
    anywhere = pl.BlockSpec(memory_space=pl.ANY)
    inputs = (in_hbm(receivers), *pieces, *map(in_hbm, (*done, split, even, odd)))
    return pl.pallas_call(
        functools.partial(lag_kernel, len(done), len(pieces), first_place, len(result)),
        out_shape=pltpu.HBM((out_rows, width), BF16),
        in_specs=[pl.BlockSpec(memory_space=pltpu.SMEM)] + [anywhere] * (len(inputs) + len(result)),
        out_specs=anywhere,
        scratch_shapes=buffers_of(inputs)
        + [
            pltpu.VMEM((2, windows, width), F32),
            pltpu.VMEM((rows, width), BF16),
            pltpu.VMEM((rows, width), BF16),
            pltpu.SemaphoreType.DMA((rows // (2 * r),)),
        ],
        input_output_aliases={len(inputs) + 1: 0} if result else {},
        compiler_params=pltpu.CompilerParams(vmem_limit_bytes=24 * 1024 * 1024),
        cost_estimate=pl.CostEstimate(flops=rows * 12 * 10**6, bytes_accessed=rows * 2**10, transcendentals=0),
        name=name,
    )(place, *inputs, *result)


def on_device(source_spectra, receiver_spectra, block_order, source_mask, receiver_mask):
    width = receiver_spectra.shape[2]
    freqs = width // 2
    r, own_windows = receiver_spectra.shape[:2]
    wins = lax.axis_size("win")
    chans = lax.axis_size("chan")
    windows = own_windows * wins
    steps = block_order.shape[0]
    me = lax.axis_index("chan")
    win = lax.axis_index("win")
    z = (me // NX) % NZ

    owned = source_spectra[0] * source_mask[0][:, None, None].astype(BF16)
    rows = owned.reshape(wins, NY, NZ, NX, own_windows, width).transpose(1, 3, 0, 2, 4, 5)
    rows = rows.reshape(NY * NX * wins, NZ * own_windows, width)
    spread = lax.all_to_all(rows, ("chan", "win"), 0, 0, tiled=True, axis_index_groups=yx_win_groups(wins))

    def all_windows(give):
        kept = [give(win)]
        for j in range(1, wins):
            kept.append(lax.ppermute(give(jnp.mod(win + j, wins)), "win", [(w, (w + j) % wins) for w in range(wins)]))
        return jnp.concatenate([lax.select_n(jnp.mod(win - w, wins), *kept) for w in range(wins)], axis=0)

    split = split_matrix(256)
    even = half_table(freqs, 0)
    odd = half_table(freqs, 1)
    ys = jnp.arange(NY, dtype=jnp.int32)
    zs = jnp.mod(z - jnp.array((0, 1, -1, 4, 2, -2, 3, -3), jnp.int32), NZ)
    bases = (jnp.arange(steps, dtype=jnp.int32)[:, None] * (NY * NZ) + (ys * NZ)[None, :]).reshape(1, -1)
    place = (bases + zs[:, None]).reshape(-1)
    owner_y, owner_z, owner_x = block_order // (NZ * NX), (block_order // NX) % NZ, block_order % NX
    first_from = [(owner_y[t] * NX + owner_x[t]) * wins for t in range(steps)]
    owner_z = [owner_z[t] for t in range(steps)]
    shadow = (split, even, odd, place, first_from, owner_z)
    spread, shadow = lax.optimization_barrier((spread, shadow))
    split, even, odd, place, first_from, owner_z = shadow

    chosen = [lax.dynamic_slice_in_dim(spread, first_from[t], wins, 0) for t in range(steps)]
    chosen = jnp.stack([part.reshape(wins, NZ, own_windows, width) for part in chosen])
    chosen = chosen.transpose(2, 0, 1, 3, 4).reshape(NZ, steps * windows, width)
    chosen = lax.all_to_all(chosen, "chan", 0, 0, tiled=True, axis_index_groups=z_groups())
    chosen = [lax.dynamic_index_in_dim(chosen, owner_z[t], 0, keepdims=False) for t in range(steps)]
    chosen = jnp.concatenate([part[t * windows : (t + 1) * windows] for t, part in enumerate(chosen)])

    def gather_yx(value):
        copies = jnp.broadcast_to(value[None], (NY * NX,) + value.shape)
        return lax.all_to_all(copies, "chan", 0, 0, tiled=True, axis_index_groups=yx_groups())

    receivers = receiver_spectra * receiver_mask[:, None, None].astype(BF16)
    receivers = all_windows(lambda to: receivers.transpose(1, 0, 2)).astype(F32)

    chosen, receivers = lax.optimization_barrier((chosen, receivers))

    near = gather_yx(chosen)
    opposite = shift(chosen, dz=4)
    near, opposite = lax.optimization_barrier((near, opposite))
    tables = (receivers, split, even, odd, steps * chans * r)
    pairs = steps * NY
    up, down = shift(near, dz=1), shift(near, dz=-1)
    cross_near = cross_of("cross_near", (near,), receivers)
    opposite, cross_near = lax.optimization_barrier((opposite, cross_near))
    far = gather_yx(opposite)
    up, down, cross_near = lax.optimization_barrier((up, down, cross_near))
    up2, down2 = shift(up, dz=1), shift(down, dz=-1)
    out = lags_of("lags_1", place, 0, (cross_near,), (up, down, far), *tables)
    up2, down2, out = lax.optimization_barrier((up2, down2, out))
    up3, down3 = shift(up2, dz=1), shift(down2, dz=-1)
    out = lags_of("lags_2", place, 4 * pairs, (), (up2, down2), *tables, out)
    up3, down3, out = lax.optimization_barrier((up3, down3, out))
    out = lags_of("lags_3", place, 6 * pairs, (), (up3, down3), *tables, out)
    return out.reshape(steps, chans, r, width)


def solution(mesh):
    return jax.shard_map(
        on_device,
        mesh=mesh,
        in_specs=(
            P("chan", None, "win", None),
            P("chan", "win", None),
            P(),
            P("chan", None),
            P("chan"),
        ),
        out_specs=P(None, "win", "chan", None),
        check_vma=False,
    )
```

```python
import functools
import math

import jax
import jax.numpy as jnp
from jax import lax
from jax.experimental import pallas as pl
from jax.experimental.pallas import tpu as pltpu
from jax.sharding import PartitionSpec as P

NY, NZ, NX = 4, 8, 2
BF16 = jnp.bfloat16
F32 = jnp.float32


def chan_index(y, z, x):
    return ((y % NY) * NZ + z % NZ) * NX + x % NX


def shift(value, dy=0, dz=0, dx=0):
    pairs = []
    for y in range(NY):
        for z in range(NZ):
            for x in range(NX):
                pairs.append((chan_index(y, z, x), chan_index(y + dy, z + dz, x + dx)))
    return lax.ppermute(value, "chan", pairs)


def yx_groups():
    return [[chan_index(y, z, x) for y in range(NY) for x in range(NX)] for z in range(NZ)]


def z_groups():
    return [[chan_index(y, z, x) for z in range(NZ)] for y in range(NY) for x in range(NX)]


def yx_win_groups(wins):
    return [[chan * wins + w for chan in group for w in range(wins)] for group in yx_groups()]


def half_table(freqs, parity):
    nfft = 2 * freqs
    bins = 2 * jnp.arange(freqs // 2, dtype=jnp.int32)[:, None] + parity
    lags = jnp.arange(freqs, dtype=jnp.int32)[None, :] - freqs
    phase = jnp.mod(bins * lags, nfft).astype(F32) * (2.0 * math.pi / nfft)
    weight = jnp.where(bins == 0, 1.0, 2.0).astype(F32) / math.sqrt(nfft)
    table = jnp.concatenate([weight * jnp.cos(phase), -weight * jnp.sin(phase)], axis=0)
    return table.astype(BF16)


def split_matrix(width):
    row = jnp.arange(width, dtype=jnp.int32)[:, None]
    column = jnp.arange(width, dtype=jnp.int32)[None, :]
    half = width // 2
    source = jnp.where(column < half, 2 * column, 2 * (column - half) + 1)
    return (row == source).astype(BF16)


def add_cross(piece, receivers, wide, cross, first_pair):
    windows, r, width = receivers.shape
    freqs = width // 2
    lane = 128
    scale = 1.0 / windows

    def one_pair(i, _, step):
        row = pl.multiple_of((first_pair + step * (piece.shape[0] // 2) + i) * 2 * r, 2 * r)
        wide[...] = piece[pl.ds(2 * i, 2), step * windows : (step + 1) * windows].astype(F32)
        for tile in range(freqs // lane):
            re = pl.ds(tile * lane, lane)
            im = pl.ds(freqs + tile * lane, lane)
            real, imag = [None, None], [None, None]
            for w in range(windows):
                c, d = receivers[w, :, re], receivers[w, :, im]
                for member in range(2):
                    a = jnp.broadcast_to(wide[member, w : w + 1, re], c.shape)
                    b = jnp.broadcast_to(wide[member, w : w + 1, im], c.shape)
                    p, q = a * c + b * d, a * d - b * c
                    real[member] = p if w == 0 else real[member] + p
                    imag[member] = q if w == 0 else imag[member] + q
            cross[pl.ds(row, 2 * r), re] = (jnp.concatenate(real) * scale).astype(BF16)
            cross[pl.ds(row, 2 * r), im] = (jnp.concatenate(imag) * scale).astype(BF16)
        return 0

    for step in range(piece.shape[1] // windows):
        lax.fori_loop(0, piece.shape[0] // 2, functools.partial(one_pair, step=step), 0)


def fetch(refs, buffers, sems):
    copies = [pltpu.make_async_copy(ref, buffer, sems.at[i]) for i, (ref, buffer) in enumerate(zip(refs, buffers))]
    for copy in copies:
        copy.start()
    return copies


def in_hbm(array):
    return pltpu.with_memory_space_constraint(array, pltpu.HBM)


def buffers_of(arrays):
    return [pltpu.VMEM(array.shape, array.dtype) for array in arrays] + [pltpu.SemaphoreType.DMA((len(arrays),))]


def cross_kernel(*refs):
    n = (len(refs) - 7) // 2
    sources, out = refs[: n + 1], refs[n + 1]
    buffers, (sems, cross, wide, sem) = refs[n + 2 : 2 * n + 3], refs[2 * n + 3 :]
    copies = fetch(sources, buffers, sems)
    copies[0].wait()
    receivers, pieces = buffers[0], buffers[1:]
    at = 0
    for piece, copy in zip(pieces, copies[1:]):
        copy.wait()
        add_cross(piece, receivers, wide, cross, at)
        at += piece.shape[0] * piece.shape[1] // (2 * receivers.shape[0])
    copy = pltpu.make_async_copy(cross, out, sem)
    copy.start()
    copy.wait()


def cross_rows(pieces, receivers):
    return sum(piece.shape[0] * piece.shape[1] for piece in pieces) * receivers.shape[1] // receivers.shape[0]


def cross_of(name, pieces, receivers):
    windows, r, width = receivers.shape
    rows = cross_rows(pieces, receivers)
    anywhere = pl.BlockSpec(memory_space=pl.ANY)
    inputs = (in_hbm(receivers), *pieces)
    return pl.pallas_call(
        cross_kernel,
        out_shape=pltpu.HBM((rows, width), BF16),
        in_specs=[anywhere] * len(inputs),
        out_specs=anywhere,
        scratch_shapes=buffers_of(inputs)
        + [pltpu.VMEM((rows, width), BF16), pltpu.VMEM((2, windows, width), F32), pltpu.SemaphoreType.DMA],
        compiler_params=pltpu.CompilerParams(vmem_limit_bytes=8 * 1024 * 1024),
        cost_estimate=pl.CostEstimate(flops=rows * 10**6, bytes_accessed=rows * 2**10, transcendentals=0),
        name=name,
    )(*inputs)


def lag_kernel(n_done, n_pieces, first_place, aliased, place, *refs):
    n = n_done + n_pieces + 4
    sources, refs = refs[:n], refs[n + aliased :]
    out, buffers, (sems, wide, cross, result, sem) = refs[0], refs[1 : n + 1], refs[n + 1 :]
    receivers, pieces, split = buffers[0], buffers[1 : 1 + n_pieces], buffers[1 + n_pieces + n_done]
    even, odd = buffers[-2:]
    spans = []
    at = 0
    pair = 2 * receivers.shape[1]
    for part in buffers[1 + n_pieces : 1 + n_pieces + n_done]:
        spans.append(cross.at[pl.ds(at * pair, part.shape[0])])
        at += part.shape[0] // pair
    targets = list(buffers)
    targets[1 + n_pieces : 1 + n_pieces + n_done] = spans
    copies = fetch(sources, targets, sems)
    copies[0].wait()
    for piece, copy in zip(pieces, copies[1:]):
        copy.wait()
        add_cross(piece, receivers, wide, cross, at)
        at += piece.shape[0] * piece.shape[1] // (2 * receivers.shape[0])
    for copy in copies[1 + n_pieces :]:
        copy.wait()
    freqs = even.shape[1]
    block = split.shape[0]
    total = at * pair
    chunk = 192 if total % 192 == 0 else 256
    copies = []
    for first in range(0, total, chunk):
        rows = pl.ds(first, chunk)
        evens, odds = [], []
        for k in range(cross.shape[1] // block):
            both = jnp.dot(cross[rows, pl.ds(k * block, block)], split[...], preferred_element_type=F32).astype(BF16)
            evens.append(both[:, : block // 2])
            odds.append(both[:, block // 2 :])
        lhs_even = jnp.concatenate(evens, axis=1)
        lhs_odd = jnp.concatenate(odds, axis=1)
        for n in range(freqs // 256):
            columns = pl.ds(n * 256, 256)
            e = jnp.dot(lhs_even, even[:, columns], preferred_element_type=F32)
            o = jnp.dot(lhs_odd, odd[:, columns], preferred_element_type=F32)
            result[rows, columns] = (e + o).astype(BF16)
            result[rows, pl.ds(freqs + n * 256, 256)] = (e - o).astype(BF16)
        for i in range(first // pair, (first + chunk) // pair):
            row = pl.multiple_of(place[first_place + i] * pair, pair)
            copy = pltpu.make_async_copy(result.at[pl.ds(i * pair, pair)], out.at[pl.ds(row, pair)], sem.at[i])
            copy.start()
            copies.append(copy)
    for copy in copies:
        copy.wait()


def lags_of(name, place, first_place, done, pieces, receivers, split, even, odd, out_rows, *result):
    windows, r, width = receivers.shape
    rows = cross_rows(pieces, receivers) + sum(part.shape[0] for part in done)
    anywhere = pl.BlockSpec(memory_space=pl.ANY)
    inputs = (in_hbm(receivers), *pieces, *map(in_hbm, (*done, split, even, odd)))
    return pl.pallas_call(
        functools.partial(lag_kernel, len(done), len(pieces), first_place, len(result)),
        out_shape=pltpu.HBM((out_rows, width), BF16),
        in_specs=[pl.BlockSpec(memory_space=pltpu.SMEM)] + [anywhere] * (len(inputs) + len(result)),
        out_specs=anywhere,
        scratch_shapes=buffers_of(inputs)
        + [
            pltpu.VMEM((2, windows, width), F32),
            pltpu.VMEM((rows, width), BF16),
            pltpu.VMEM((rows, width), BF16),
            pltpu.SemaphoreType.DMA((rows // (2 * r),)),
        ],
        input_output_aliases={len(inputs) + 1: 0} if result else {},
        compiler_params=pltpu.CompilerParams(vmem_limit_bytes=24 * 1024 * 1024),
        cost_estimate=pl.CostEstimate(flops=rows * 12 * 10**6, bytes_accessed=rows * 2**10, transcendentals=0),
        name=name,
    )(place, *inputs, *result)


def on_device(source_spectra, receiver_spectra, block_order, source_mask, receiver_mask):
    width = receiver_spectra.shape[2]
    freqs = width // 2
    r, own_windows = receiver_spectra.shape[:2]
    wins = lax.axis_size("win")
    chans = lax.axis_size("chan")
    windows = own_windows * wins
    steps = block_order.shape[0]
    me = lax.axis_index("chan")
    win = lax.axis_index("win")
    z = (me // NX) % NZ

    owned = source_spectra[0] * source_mask[0][:, None, None].astype(BF16)
    rows = owned.reshape(wins, NY, NZ, NX, own_windows, width).transpose(1, 3, 0, 2, 4, 5)
    rows = rows.reshape(NY * NX * wins, NZ * own_windows, width)
    spread = lax.all_to_all(rows, ("chan", "win"), 0, 0, tiled=True, axis_index_groups=yx_win_groups(wins))

    def all_windows(give):
        kept = [give(win)]
        for j in range(1, wins):
            kept.append(lax.ppermute(give(jnp.mod(win + j, wins)), "win", [(w, (w + j) % wins) for w in range(wins)]))
        return jnp.concatenate([lax.select_n(jnp.mod(win - w, wins), *kept) for w in range(wins)], axis=0)

    split = split_matrix(256)
    even = half_table(freqs, 0)
    odd = half_table(freqs, 1)
    ys = jnp.arange(NY, dtype=jnp.int32)
    zs = jnp.mod(z - jnp.array((0, 1, -1, 4, 2, -2, 3, -3), jnp.int32), NZ)
    bases = (jnp.arange(steps, dtype=jnp.int32)[:, None] * (NY * NZ) + (ys * NZ)[None, :]).reshape(1, -1)
    place = (bases + zs[:, None]).reshape(-1)
    owner_y, owner_z, owner_x = block_order // (NZ * NX), (block_order // NX) % NZ, block_order % NX
    first_from = [(owner_y[t] * NX + owner_x[t]) * wins for t in range(steps)]
    owner_z = [owner_z[t] for t in range(steps)]
    shadow = (split, even, odd, place, first_from, owner_z)
    spread, shadow = lax.optimization_barrier((spread, shadow))
    split, even, odd, place, first_from, owner_z = shadow

    chosen = [lax.dynamic_slice_in_dim(spread, first_from[t], wins, 0) for t in range(steps)]
    chosen = jnp.stack([part.reshape(wins, NZ, own_windows, width) for part in chosen])
    chosen = chosen.transpose(2, 0, 1, 3, 4).reshape(NZ, steps * windows, width)
    chosen = lax.all_to_all(chosen, "chan", 0, 0, tiled=True, axis_index_groups=z_groups())
    chosen = [lax.dynamic_index_in_dim(chosen, owner_z[t], 0, keepdims=False) for t in range(steps)]
    chosen = jnp.concatenate([part[t * windows : (t + 1) * windows] for t, part in enumerate(chosen)])

    def gather_yx(value):
        copies = jnp.broadcast_to(value[None], (NY * NX,) + value.shape)
        return lax.all_to_all(copies, "chan", 0, 0, tiled=True, axis_index_groups=yx_groups())

    receivers = receiver_spectra * receiver_mask[:, None, None].astype(BF16)
    receivers = all_windows(lambda to: receivers.transpose(1, 0, 2)).astype(F32)

    chosen, receivers = lax.optimization_barrier((chosen, receivers))

    near = gather_yx(chosen)
    opposite = shift(chosen, dz=4)
    tables = (receivers, split, even, odd, steps * chans * r)
    pairs = steps * NY
    near, opposite = lax.optimization_barrier((near, opposite))
    up, down = shift(near, dz=1), shift(near, dz=-1)
    ready = near
    cross_near = cross_of("cross_near", (ready,), receivers)
    opposite, cross_near = lax.optimization_barrier((opposite, cross_near))
    far = gather_yx(opposite)
    up, down, cross_near = lax.optimization_barrier((up, down, cross_near))
    up2, down2 = shift(up, dz=1), shift(down, dz=-1)
    far, cross_near = lax.optimization_barrier((far, cross_near))
    out = lags_of("lags_1", place, 0, (cross_near,), (up, down), *tables)
    up2, down2, out = lax.optimization_barrier((up2, down2, out))
    up3, down3 = shift(up2, dz=1), shift(down2, dz=-1)
    out = lags_of("lags_2", place, 3 * pairs, (), (far, up2, down2), *tables, out)
    up3, down3, out = lax.optimization_barrier((up3, down3, out))
    out = lags_of("lags_3", place, 6 * pairs, (), (up3, down3), *tables, out)
    return out.reshape(steps, chans, r, width)


def solution(mesh):
    return jax.shard_map(
        on_device,
        mesh=mesh,
        in_specs=(
            P("chan", None, "win", None),
            P("chan", "win", None),
            P(),
            P("chan", None),
            P("chan"),
        ),
        out_specs=P(None, "win", "chan", None),
        check_vma=False,
    )
```

```python
import functools
import math

import jax
import jax.numpy as jnp
from jax import lax
from jax.experimental import pallas as pl
from jax.experimental.pallas import tpu as pltpu
from jax.sharding import PartitionSpec as P

NY, NZ, NX = 4, 8, 2
BF16 = jnp.bfloat16
F32 = jnp.float32


def chan_index(y, z, x):
    return ((y % NY) * NZ + z % NZ) * NX + x % NX


def shift(value, dy=0, dz=0, dx=0):
    pairs = []
    for y in range(NY):
        for z in range(NZ):
            for x in range(NX):
                pairs.append((chan_index(y, z, x), chan_index(y + dy, z + dz, x + dx)))
    return lax.ppermute(value, "chan", pairs)


def yx_groups():
    return [[chan_index(y, z, x) for y in range(NY) for x in range(NX)] for z in range(NZ)]


def z_groups():
    return [[chan_index(y, z, x) for z in range(NZ)] for y in range(NY) for x in range(NX)]


def yx_win_groups(wins):
    return [[chan * wins + w for chan in group for w in range(wins)] for group in yx_groups()]


def half_table(freqs, parity):
    nfft = 2 * freqs
    bins = 2 * jnp.arange(freqs // 2, dtype=jnp.int32)[:, None] + parity
    lags = jnp.arange(freqs, dtype=jnp.int32)[None, :] - freqs
    phase = jnp.mod(bins * lags, nfft).astype(F32) * (2.0 * math.pi / nfft)
    weight = jnp.where(bins == 0, 1.0, 2.0).astype(F32) / math.sqrt(nfft)
    table = jnp.concatenate([weight * jnp.cos(phase), -weight * jnp.sin(phase)], axis=0)
    return table.astype(BF16)


def split_matrix(width):
    row = jnp.arange(width, dtype=jnp.int32)[:, None]
    column = jnp.arange(width, dtype=jnp.int32)[None, :]
    half = width // 2
    source = jnp.where(column < half, 2 * column, 2 * (column - half) + 1)
    return (row == source).astype(BF16)


def add_cross(piece, receivers, wide, cross, first_pair):
    windows, r, width = receivers.shape
    freqs = width // 2
    lane = 128
    scale = 1.0 / windows

    def one_pair(i, _, step):
        row = pl.multiple_of((first_pair + step * (piece.shape[0] // 2) + i) * 2 * r, 2 * r)
        wide[...] = piece[pl.ds(2 * i, 2), step * windows : (step + 1) * windows].astype(F32)
        for tile in range(freqs // lane):
            re = pl.ds(tile * lane, lane)
            im = pl.ds(freqs + tile * lane, lane)
            real, imag = [None, None], [None, None]
            for w in range(windows):
                c, d = receivers[w, :, re], receivers[w, :, im]
                for member in range(2):
                    a = jnp.broadcast_to(wide[member, w : w + 1, re], c.shape)
                    b = jnp.broadcast_to(wide[member, w : w + 1, im], c.shape)
                    p, q = a * c + b * d, a * d - b * c
                    real[member] = p if w == 0 else real[member] + p
                    imag[member] = q if w == 0 else imag[member] + q
            cross[pl.ds(row, 2 * r), re] = (jnp.concatenate(real) * scale).astype(BF16)
            cross[pl.ds(row, 2 * r), im] = (jnp.concatenate(imag) * scale).astype(BF16)
        return 0

    for step in range(piece.shape[1] // windows):
        lax.fori_loop(0, piece.shape[0] // 2, functools.partial(one_pair, step=step), 0)


def fetch(refs, buffers, sems):
    copies = [pltpu.make_async_copy(ref, buffer, sems.at[i]) for i, (ref, buffer) in enumerate(zip(refs, buffers))]
    for copy in copies:
        copy.start()
    return copies


def in_hbm(array):
    return pltpu.with_memory_space_constraint(array, pltpu.HBM)


def buffers_of(arrays):
    return [pltpu.VMEM(array.shape, array.dtype) for array in arrays] + [pltpu.SemaphoreType.DMA((len(arrays),))]


def cross_kernel(*refs):
    n = (len(refs) - 7) // 2
    sources, out = refs[: n + 1], refs[n + 1]
    buffers, (sems, cross, wide, sem) = refs[n + 2 : 2 * n + 3], refs[2 * n + 3 :]
    copies = fetch(sources, buffers, sems)
    copies[0].wait()
    receivers, pieces = buffers[0], buffers[1:]
    at = 0
    for piece, copy in zip(pieces, copies[1:]):
        copy.wait()
        add_cross(piece, receivers, wide, cross, at)
        at += piece.shape[0] * piece.shape[1] // (2 * receivers.shape[0])
    copy = pltpu.make_async_copy(cross, out, sem)
    copy.start()
    copy.wait()


def cross_rows(pieces, receivers):
    return sum(piece.shape[0] * piece.shape[1] for piece in pieces) * receivers.shape[1] // receivers.shape[0]


def cross_of(name, pieces, receivers):
    windows, r, width = receivers.shape
    rows = cross_rows(pieces, receivers)
    anywhere = pl.BlockSpec(memory_space=pl.ANY)
    inputs = (in_hbm(receivers), *pieces)
    return pl.pallas_call(
        cross_kernel,
        out_shape=pltpu.HBM((rows, width), BF16),
        in_specs=[anywhere] * len(inputs),
        out_specs=anywhere,
        scratch_shapes=buffers_of(inputs)
        + [pltpu.VMEM((rows, width), BF16), pltpu.VMEM((2, windows, width), F32), pltpu.SemaphoreType.DMA],
        compiler_params=pltpu.CompilerParams(vmem_limit_bytes=8 * 1024 * 1024),
        cost_estimate=pl.CostEstimate(flops=rows * 10**6, bytes_accessed=rows * 2**10, transcendentals=0),
        name=name,
    )(*inputs)


def lag_kernel(n_done, n_pieces, first_place, aliased, place, *refs):
    n = n_done + n_pieces + 4
    sources, refs = refs[:n], refs[n + aliased :]
    out, buffers, (sems, wide, cross, result, sem) = refs[0], refs[1 : n + 1], refs[n + 1 :]
    receivers, pieces, split = buffers[0], buffers[1 : 1 + n_pieces], buffers[1 + n_pieces + n_done]
    even, odd = buffers[-2:]
    spans = []
    at = 0
    pair = 2 * receivers.shape[1]
    for part in buffers[1 + n_pieces : 1 + n_pieces + n_done]:
        spans.append(cross.at[pl.ds(at * pair, part.shape[0])])
        at += part.shape[0] // pair
    targets = list(buffers)
    targets[1 + n_pieces : 1 + n_pieces + n_done] = spans
    copies = [pltpu.make_async_copy(ref, target, sems.at[i]) for i, (ref, target) in enumerate(zip(sources, targets))]
    for copy in copies[: 1 + n_pieces]:
        copy.start()
    copies[0].wait()
    for number, (piece, copy) in enumerate(zip(pieces, copies[1:])):
        copy.wait()
        if number == 0:
            for later in copies[1 + n_pieces :]:
                later.start()
        add_cross(piece, receivers, wide, cross, at)
        at += piece.shape[0] * piece.shape[1] // (2 * receivers.shape[0])
    for copy in copies[1 + n_pieces :]:
        copy.wait()
    freqs = even.shape[1]
    block = split.shape[0]
    total = at * pair
    chunk = 192 if total % 192 == 0 else 256
    copies = []
    for first in range(0, total, chunk):
        rows = pl.ds(first, chunk)
        evens, odds = [], []
        for k in range(cross.shape[1] // block):
            both = jnp.dot(cross[rows, pl.ds(k * block, block)], split[...], preferred_element_type=F32).astype(BF16)
            evens.append(both[:, : block // 2])
            odds.append(both[:, block // 2 :])
        lhs_even = jnp.concatenate(evens, axis=1)
        lhs_odd = jnp.concatenate(odds, axis=1)
        for n in range(freqs // 256):
            columns = pl.ds(n * 256, 256)
            e = jnp.dot(lhs_even, even[:, columns], preferred_element_type=F32)
            o = jnp.dot(lhs_odd, odd[:, columns], preferred_element_type=F32)
            result[rows, columns] = (e + o).astype(BF16)
            result[rows, pl.ds(freqs + n * 256, 256)] = (e - o).astype(BF16)
        for i in range(first // pair, (first + chunk) // pair):
            row = pl.multiple_of(place[first_place + i] * pair, pair)
            copy = pltpu.make_async_copy(result.at[pl.ds(i * pair, pair)], out.at[pl.ds(row, pair)], sem.at[i])
            copy.start()
            copies.append(copy)
    for copy in copies:
        copy.wait()


def lags_of(name, place, first_place, done, pieces, receivers, split, even, odd, out_rows, *result):
    windows, r, width = receivers.shape
    rows = cross_rows(pieces, receivers) + sum(part.shape[0] for part in done)
    anywhere = pl.BlockSpec(memory_space=pl.ANY)
    inputs = (in_hbm(receivers), *pieces, *map(in_hbm, (*done, split, even, odd)))
    return pl.pallas_call(
        functools.partial(lag_kernel, len(done), len(pieces), first_place, len(result)),
        out_shape=pltpu.HBM((out_rows, width), BF16),
        in_specs=[pl.BlockSpec(memory_space=pltpu.SMEM)] + [anywhere] * (len(inputs) + len(result)),
        out_specs=anywhere,
        scratch_shapes=buffers_of(inputs)
        + [
            pltpu.VMEM((2, windows, width), F32),
            pltpu.VMEM((rows, width), BF16),
            pltpu.VMEM((rows, width), BF16),
            pltpu.SemaphoreType.DMA((rows // (2 * r),)),
        ],
        input_output_aliases={len(inputs) + 1: 0} if result else {},
        compiler_params=pltpu.CompilerParams(vmem_limit_bytes=24 * 1024 * 1024),
        cost_estimate=pl.CostEstimate(flops=rows * 12 * 10**6, bytes_accessed=rows * 2**10, transcendentals=0),
        name=name,
    )(place, *inputs, *result)


def on_device(source_spectra, receiver_spectra, block_order, source_mask, receiver_mask):
    width = receiver_spectra.shape[2]
    freqs = width // 2
    r, own_windows = receiver_spectra.shape[:2]
    wins = lax.axis_size("win")
    chans = lax.axis_size("chan")
    windows = own_windows * wins
    steps = block_order.shape[0]
    me = lax.axis_index("chan")
    win = lax.axis_index("win")
    z = (me // NX) % NZ

    owned = source_spectra[0] * source_mask[0][:, None, None].astype(BF16)
    rows = owned.reshape(wins, NY, NZ, NX, own_windows, width).transpose(1, 3, 0, 2, 4, 5)
    rows = rows.reshape(NY * NX * wins, NZ * own_windows, width)
    spread = lax.all_to_all(rows, ("chan", "win"), 0, 0, tiled=True, axis_index_groups=yx_win_groups(wins))

    def all_windows(give):
        kept = [give(win)]
        for j in range(1, wins):
            kept.append(lax.ppermute(give(jnp.mod(win + j, wins)), "win", [(w, (w + j) % wins) for w in range(wins)]))
        return jnp.concatenate([lax.select_n(jnp.mod(win - w, wins), *kept) for w in range(wins)], axis=0)

    split = split_matrix(256)
    even = half_table(freqs, 0)
    odd = half_table(freqs, 1)
    ys = jnp.arange(NY, dtype=jnp.int32)
    zs = jnp.mod(z - jnp.array((0, 1, -1, 4, 2, -2, 3, -3), jnp.int32), NZ)
    bases = (jnp.arange(steps, dtype=jnp.int32)[:, None] * (NY * NZ) + (ys * NZ)[None, :]).reshape(1, -1)
    place = (bases + zs[:, None]).reshape(-1)
    owner_y, owner_z, owner_x = block_order // (NZ * NX), (block_order // NX) % NZ, block_order % NX
    first_from = [(owner_y[t] * NX + owner_x[t]) * wins for t in range(steps)]
    owner_z = [owner_z[t] for t in range(steps)]
    shadow = (split, even, odd, place, first_from, owner_z)
    spread, shadow = lax.optimization_barrier((spread, shadow))
    split, even, odd, place, first_from, owner_z = shadow

    chosen = [lax.dynamic_slice_in_dim(spread, first_from[t], wins, 0) for t in range(steps)]
    chosen = jnp.stack([part.reshape(wins, NZ, own_windows, width) for part in chosen])
    chosen = chosen.transpose(2, 0, 1, 3, 4).reshape(NZ, steps * windows, width)
    chosen = lax.all_to_all(chosen, "chan", 0, 0, tiled=True, axis_index_groups=z_groups())
    chosen = [lax.dynamic_index_in_dim(chosen, owner_z[t], 0, keepdims=False) for t in range(steps)]
    chosen = jnp.concatenate([part[t * windows : (t + 1) * windows] for t, part in enumerate(chosen)])

    def gather_yx(value):
        copies = jnp.broadcast_to(value[None], (NY * NX,) + value.shape)
        return lax.all_to_all(copies, "chan", 0, 0, tiled=True, axis_index_groups=yx_groups())

    receivers = receiver_spectra * receiver_mask[:, None, None].astype(BF16)
    receivers = all_windows(lambda to: receivers.transpose(1, 0, 2)).astype(F32)

    chosen, receivers = lax.optimization_barrier((chosen, receivers))

    near = gather_yx(chosen)
    opposite = shift(chosen, dz=4)
    tables = (receivers, split, even, odd, steps * chans * r)
    pairs = steps * NY
    near, opposite = lax.optimization_barrier((near, opposite))
    up, down = shift(near, dz=1), shift(near, dz=-1)
    ready = near
    cross_near = cross_of("cross_near", (ready,), receivers)
    opposite, cross_near = lax.optimization_barrier((opposite, cross_near))
    far = gather_yx(opposite)
    up, down, cross_near = lax.optimization_barrier((up, down, cross_near))
    up2, down2 = shift(up, dz=1), shift(down, dz=-1)
    far, cross_near = lax.optimization_barrier((far, cross_near))
    out = lags_of("lags_1", place, 0, (cross_near,), (up, down), *tables)
    up2, down2, out = lax.optimization_barrier((up2, down2, out))
    up3, down3 = shift(up2, dz=1), shift(down2, dz=-1)
    out = lags_of("lags_2", place, 3 * pairs, (), (far, up2, down2), *tables, out)
    up3, down3, out = lax.optimization_barrier((up3, down3, out))
    out = lags_of("lags_3", place, 6 * pairs, (), (up3, down3), *tables, out)
    return out.reshape(steps, chans, r, width)


def solution(mesh):
    return jax.shard_map(
        on_device,
        mesh=mesh,
        in_specs=(
            P("chan", None, "win", None),
            P("chan", "win", None),
            P(),
            P("chan", None),
            P("chan"),
        ),
        out_specs=P(None, "win", "chan", None),
        check_vma=False,
    )
```

```python
import functools
import math

import jax
import jax.numpy as jnp
from jax import lax
from jax.experimental import pallas as pl
from jax.experimental.pallas import tpu as pltpu
from jax.sharding import PartitionSpec as P

NY, NZ, NX = 4, 8, 2
BF16 = jnp.bfloat16
F32 = jnp.float32


def chan_index(y, z, x):
    return ((y % NY) * NZ + z % NZ) * NX + x % NX


def shift(value, dy=0, dz=0, dx=0):
    pairs = []
    for y in range(NY):
        for z in range(NZ):
            for x in range(NX):
                pairs.append((chan_index(y, z, x), chan_index(y + dy, z + dz, x + dx)))
    return lax.ppermute(value, "chan", pairs)


def yx_groups():
    return [[chan_index(y, z, x) for y in range(NY) for x in range(NX)] for z in range(NZ)]


def z_groups():
    return [[chan_index(y, z, x) for z in range(NZ)] for y in range(NY) for x in range(NX)]


def yx_win_groups(wins):
    return [[chan * wins + w for chan in group for w in range(wins)] for group in yx_groups()]


def half_table(freqs, parity):
    nfft = 2 * freqs
    bins = 2 * jnp.arange(freqs // 2, dtype=jnp.int32)[:, None] + parity
    lags = jnp.arange(freqs, dtype=jnp.int32)[None, :] - freqs
    phase = jnp.mod(bins * lags, nfft).astype(F32) * (2.0 * math.pi / nfft)
    weight = jnp.where(bins == 0, 1.0, 2.0).astype(F32) / math.sqrt(nfft)
    table = jnp.concatenate([weight * jnp.cos(phase), -weight * jnp.sin(phase)], axis=0)
    return table.astype(BF16)


def split_matrix(width):
    row = jnp.arange(width, dtype=jnp.int32)[:, None]
    column = jnp.arange(width, dtype=jnp.int32)[None, :]
    half = width // 2
    source = jnp.where(column < half, 2 * column, 2 * (column - half) + 1)
    return (row == source).astype(BF16)


def add_cross(piece, receivers, wide, cross, first_pair):
    windows, r, width = receivers.shape
    freqs = width // 2
    lane = 128
    scale = 1.0 / windows

    members = wide.shape[0]

    def one_group(i, _, step):
        pairs = members // 2
        row = pl.multiple_of((first_pair + step * (piece.shape[0] // 2) + i * pairs) * 2 * r, 2 * r)
        wide[...] = piece[pl.ds(members * i, members), step * windows : (step + 1) * windows].astype(F32)
        for tile in range(freqs // lane):
            re = pl.ds(tile * lane, lane)
            im = pl.ds(freqs + tile * lane, lane)
            real, imag = [None] * members, [None] * members
            for w in range(windows):
                c, d = receivers[w, :, re], receivers[w, :, im]
                for member in range(members):
                    a = jnp.broadcast_to(wide[member, w : w + 1, re], c.shape)
                    b = jnp.broadcast_to(wide[member, w : w + 1, im], c.shape)
                    p, q = a * c + b * d, a * d - b * c
                    real[member] = p if w == 0 else real[member] + p
                    imag[member] = q if w == 0 else imag[member] + q
            for n in range(pairs):
                rows = pl.ds(pl.multiple_of(row + n * 2 * r, 2 * r), 2 * r)
                cross[rows, re] = (jnp.concatenate(real[2 * n : 2 * n + 2]) * scale).astype(BF16)
                cross[rows, im] = (jnp.concatenate(imag[2 * n : 2 * n + 2]) * scale).astype(BF16)
        return 0

    for step in range(piece.shape[1] // windows):
        lax.fori_loop(0, piece.shape[0] // members, functools.partial(one_group, step=step), 0)


def fetch(refs, buffers, sems):
    copies = [pltpu.make_async_copy(ref, buffer, sems.at[i]) for i, (ref, buffer) in enumerate(zip(refs, buffers))]
    for copy in copies:
        copy.start()
    return copies


def in_hbm(array):
    return pltpu.with_memory_space_constraint(array, pltpu.HBM)


def buffers_of(arrays):
    return [pltpu.VMEM(array.shape, array.dtype) for array in arrays] + [pltpu.SemaphoreType.DMA((len(arrays),))]


def cross_kernel(*refs):
    n = (len(refs) - 7) // 2
    sources, out = refs[: n + 1], refs[n + 1]
    buffers, (sems, cross, wide, sem) = refs[n + 2 : 2 * n + 3], refs[2 * n + 3 :]
    copies = fetch(sources, buffers, sems)
    copies[0].wait()
    receivers, pieces = buffers[0], buffers[1:]
    at = 0
    for piece, copy in zip(pieces, copies[1:]):
        copy.wait()
        add_cross(piece, receivers, wide, cross, at)
        at += piece.shape[0] * piece.shape[1] // (2 * receivers.shape[0])
    copy = pltpu.make_async_copy(cross, out, sem)
    copy.start()
    copy.wait()


def cross_rows(pieces, receivers):
    return sum(piece.shape[0] * piece.shape[1] for piece in pieces) * receivers.shape[1] // receivers.shape[0]


def cross_of(name, pieces, receivers):
    windows, r, width = receivers.shape
    rows = cross_rows(pieces, receivers)
    anywhere = pl.BlockSpec(memory_space=pl.ANY)
    inputs = (in_hbm(receivers), *pieces)
    return pl.pallas_call(
        cross_kernel,
        out_shape=pltpu.HBM((rows, width), BF16),
        in_specs=[anywhere] * len(inputs),
        out_specs=anywhere,
        scratch_shapes=buffers_of(inputs)
        + [pltpu.VMEM((rows, width), BF16), pltpu.VMEM((4, windows, width), F32), pltpu.SemaphoreType.DMA],
        compiler_params=pltpu.CompilerParams(vmem_limit_bytes=8 * 1024 * 1024),
        cost_estimate=pl.CostEstimate(flops=rows * 10**6, bytes_accessed=rows * 2**10, transcendentals=0),
        name=name,
    )(*inputs)


def lag_kernel(n_done, n_pieces, first_place, aliased, place, *refs):
    n = n_done + n_pieces + 4
    sources, refs = refs[:n], refs[n + aliased :]
    out, buffers, (sems, wide, cross, result, sem) = refs[0], refs[1 : n + 1], refs[n + 1 :]
    receivers, pieces, split = buffers[0], buffers[1 : 1 + n_pieces], buffers[1 + n_pieces + n_done]
    even, odd = buffers[-2:]
    spans = []
    at = 0
    pair = 2 * receivers.shape[1]
    for part in buffers[1 + n_pieces : 1 + n_pieces + n_done]:
        spans.append(cross.at[pl.ds(at * pair, part.shape[0])])
        at += part.shape[0] // pair
    targets = list(buffers)
    targets[1 + n_pieces : 1 + n_pieces + n_done] = spans
    copies = fetch(sources, targets, sems)
    copies[0].wait()
    for piece, copy in zip(pieces, copies[1:]):
        copy.wait()
        add_cross(piece, receivers, wide, cross, at)
        at += piece.shape[0] * piece.shape[1] // (2 * receivers.shape[0])
    for copy in copies[1 + n_pieces :]:
        copy.wait()
    freqs = even.shape[1]
    block = split.shape[0]
    total = at * pair
    chunk = 192 if total % 192 == 0 else 128
    copies = []
    for first in range(0, total, chunk):
        rows = pl.ds(first, chunk)
        evens, odds = [], []
        for k in range(cross.shape[1] // block):
            both = jnp.dot(cross[rows, pl.ds(k * block, block)], split[...], preferred_element_type=F32).astype(BF16)
            evens.append(both[:, : block // 2])
            odds.append(both[:, block // 2 :])
        lhs_even = jnp.concatenate(evens, axis=1)
        lhs_odd = jnp.concatenate(odds, axis=1)
        for n in range(freqs // 256):
            columns = pl.ds(n * 256, 256)
            e = jnp.dot(lhs_even, even[:, columns], preferred_element_type=F32)
            o = jnp.dot(lhs_odd, odd[:, columns], preferred_element_type=F32)
            result[rows, columns] = (e + o).astype(BF16)
            result[rows, pl.ds(freqs + n * 256, 256)] = (e - o).astype(BF16)
        for i in range(first // pair, (first + chunk) // pair):
            row = pl.multiple_of(place[first_place + i] * pair, pair)
            copy = pltpu.make_async_copy(result.at[pl.ds(i * pair, pair)], out.at[pl.ds(row, pair)], sem.at[i])
            copy.start()
            copies.append(copy)
    for copy in copies:
        copy.wait()


def lags_of(name, place, first_place, done, pieces, receivers, split, even, odd, out_rows, *result):
    windows, r, width = receivers.shape
    rows = cross_rows(pieces, receivers) + sum(part.shape[0] for part in done)
    anywhere = pl.BlockSpec(memory_space=pl.ANY)
    inputs = (in_hbm(receivers), *pieces, *map(in_hbm, (*done, split, even, odd)))
    return pl.pallas_call(
        functools.partial(lag_kernel, len(done), len(pieces), first_place, len(result)),
        out_shape=pltpu.HBM((out_rows, width), BF16),
        in_specs=[pl.BlockSpec(memory_space=pltpu.SMEM)] + [anywhere] * (len(inputs) + len(result)),
        out_specs=anywhere,
        scratch_shapes=buffers_of(inputs)
        + [
            pltpu.VMEM((4, windows, width), F32),
            pltpu.VMEM((rows, width), BF16),
            pltpu.VMEM((rows, width), BF16),
            pltpu.SemaphoreType.DMA((rows // (2 * r),)),
        ],
        input_output_aliases={len(inputs) + 1: 0} if result else {},
        compiler_params=pltpu.CompilerParams(vmem_limit_bytes=24 * 1024 * 1024),
        cost_estimate=pl.CostEstimate(flops=rows * 12 * 10**6, bytes_accessed=rows * 2**10, transcendentals=0),
        name=name,
    )(place, *inputs, *result)


def on_device(source_spectra, receiver_spectra, block_order, source_mask, receiver_mask):
    width = receiver_spectra.shape[2]
    freqs = width // 2
    r, own_windows = receiver_spectra.shape[:2]
    wins = lax.axis_size("win")
    chans = lax.axis_size("chan")
    windows = own_windows * wins
    steps = block_order.shape[0]
    me = lax.axis_index("chan")
    win = lax.axis_index("win")
    z = (me // NX) % NZ

    owned = source_spectra[0] * source_mask[0][:, None, None].astype(BF16)
    rows = owned.reshape(wins, NY, NZ, NX, own_windows, width).transpose(1, 3, 0, 2, 4, 5)
    rows = rows.reshape(NY * NX * wins, NZ * own_windows, width)
    spread = lax.all_to_all(rows, ("chan", "win"), 0, 0, tiled=True, axis_index_groups=yx_win_groups(wins))

    def all_windows(give):
        kept = [give(win)]
        for j in range(1, wins):
            kept.append(lax.ppermute(give(jnp.mod(win + j, wins)), "win", [(w, (w + j) % wins) for w in range(wins)]))
        return jnp.concatenate([lax.select_n(jnp.mod(win - w, wins), *kept) for w in range(wins)], axis=0)

    split = split_matrix(256)
    even = half_table(freqs, 0)
    odd = half_table(freqs, 1)
    ys = jnp.arange(NY, dtype=jnp.int32)
    zs = jnp.mod(z - jnp.array((0, 1, -1, 4, 2, -2, 3, -3), jnp.int32), NZ)
    bases = (jnp.arange(steps, dtype=jnp.int32)[:, None] * (NY * NZ) + (ys * NZ)[None, :]).reshape(1, -1)
    place = (bases + zs[:, None]).reshape(-1)
    owner_y, owner_z, owner_x = block_order // (NZ * NX), (block_order // NX) % NZ, block_order % NX
    first_from = [(owner_y[t] * NX + owner_x[t]) * wins for t in range(steps)]
    owner_z = [owner_z[t] for t in range(steps)]
    shadow = (split, even, odd, place, first_from, owner_z)
    spread, shadow = lax.optimization_barrier((spread, shadow))
    split, even, odd, place, first_from, owner_z = shadow

    chosen = [lax.dynamic_slice_in_dim(spread, first_from[t], wins, 0) for t in range(steps)]
    chosen = jnp.stack([part.reshape(wins, NZ, own_windows, width) for part in chosen])
    chosen = chosen.transpose(2, 0, 1, 3, 4).reshape(NZ, steps * windows, width)
    chosen = lax.all_to_all(chosen, "chan", 0, 0, tiled=True, axis_index_groups=z_groups())
    chosen = [lax.dynamic_index_in_dim(chosen, owner_z[t], 0, keepdims=False) for t in range(steps)]
    chosen = jnp.concatenate([part[t * windows : (t + 1) * windows] for t, part in enumerate(chosen)])

    def gather_yx(value):
        copies = jnp.broadcast_to(value[None], (NY * NX,) + value.shape)
        return lax.all_to_all(copies, "chan", 0, 0, tiled=True, axis_index_groups=yx_groups())

    receivers = receiver_spectra * receiver_mask[:, None, None].astype(BF16)
    receivers = all_windows(lambda to: receivers.transpose(1, 0, 2)).astype(F32)

    chosen, receivers = lax.optimization_barrier((chosen, receivers))

    near = gather_yx(chosen)
    opposite = shift(chosen, dz=4)
    tables = (receivers, split, even, odd, steps * chans * r)
    pairs = steps * NY
    near, opposite = lax.optimization_barrier((near, opposite))
    up, down = shift(near, dz=1), shift(near, dz=-1)
    ready = near
    cross_near = cross_of("cross_near", (ready,), receivers)
    opposite, cross_near = lax.optimization_barrier((opposite, cross_near))
    far = gather_yx(opposite)
    up, down, cross_near = lax.optimization_barrier((up, down, cross_near))
    up2, down2 = shift(up, dz=1), shift(down, dz=-1)
    far, cross_near = lax.optimization_barrier((far, cross_near))
    out = lags_of("lags_1", place, 0, (cross_near,), (up, down), *tables)
    up2, down2, out = lax.optimization_barrier((up2, down2, out))
    up3, down3 = shift(up2, dz=1), shift(down2, dz=-1)
    out = lags_of("lags_2", place, 3 * pairs, (), (far, up2, down2), *tables, out)
    up3, down3, out = lax.optimization_barrier((up3, down3, out))
    out = lags_of("lags_3", place, 6 * pairs, (), (up3, down3), *tables, out)
    return out.reshape(steps, chans, r, width)


def solution(mesh):
    return jax.shard_map(
        on_device,
        mesh=mesh,
        in_specs=(
            P("chan", None, "win", None),
            P("chan", "win", None),
            P(),
            P("chan", None),
            P("chan"),
        ),
        out_specs=P(None, "win", "chan", None),
        check_vma=False,
    )
```
